32 devices in a mesh: groups: 2 (over y), row: 4 (over z), col: 4 (over x, core).
Axes of the slice: x: 2, y: 2, z: 4, core: 2. Of those that a mesh axis runs over, the one named last changes fastest.
Arguments:
- pair: bfloat16 [512, 256, 128], P(('groups', 'row'), 'col'), parts along dimension 0, may hold values from -6 to 6
- mask: int32 [512], P('groups'), parts along dimension 0, may hold values 0 or 1
- ln_gain: float32 [128], replicated, may hold values from 0.5 to 2
- ln_bias: float32 [128], replicated, may hold values from -3 to 3
- w_left: bfloat16 [128, 256], replicated, may hold values from -0.5 to 0.5
- w_right: bfloat16 [128, 256], replicated, may hold values from -0.5 to 0.5
- w_gate: bfloat16 [128, 128], replicated, may hold values from -0.5 to 0.5
- w_out: bfloat16 [128, 128], replicated, may hold values from -0.5 to 0.5
- out_gain: float32 [128], replicated, may hold values from 0.5 to 2
- out_bias: float32 [128], replicated, may hold values from -3 to 3
Outputs:
- update: bfloat16 [512, 256, 128], P(('groups', 'row'), 'col'), parts along dimension 0
The draws below stay inside these ranges and needn't reach their ends.
There are 2 independent parts, one for each index of `groups`. The reference program is written for one: setup_inputs(seed, part) draws one part's arguments, and reference() takes and returns one part's arrays. A program takes and returns all parts, laid end to end along the dimension named above; an argument that names none is the same for every part. Nothing has to cross between parts.
Inputs may be any that keep to these rules, and one draw needn't show every extreme that they name: `mask`: 1 marks a valid token.
All inputs are finite; a program needn't handle non-finite values.
Results may differ from the reference program's by a relative error of at most 0.0059.
Values may be sent and summed in bfloat16 or wider, within the bound.
A program may use at most 64 MiB of HBM per device.

```python
import math
import jax
import jax.numpy as jnp
from jax import lax

C = 128
CH = 128
N_TOK = 256


def plant(values, stream_key, smallest, top_value):
    spot = [jax.random.randint(jax.random.fold_in(stream_key, axis), (), 0, length) for axis, length in enumerate(values.shape)]
    longest = values.shape.index(max(values.shape))
    next_to = spot[:longest] + [(spot[longest] + 1) % values.shape[longest]] + spot[longest + 1:]
    return values.at[tuple(spot)].set(smallest).at[tuple(next_to)].set(top_value)


def block_levels(stream_key, dims, shards, least, largest):
    def one(axis_at, blocks):
        draws = jax.random.uniform(jax.random.fold_in(jax.random.fold_in(stream_key, 6), axis_at), (blocks,), jnp.float32, least / len(shards), largest / len(shards))
        return jnp.repeat(jnp.exp(draws), dims[axis_at] // blocks).reshape((-1,) + (1,) * (len(dims) - axis_at - 1))

    level = one(*shards[0])
    for cut in shards[1:]:
        level = level * one(*cut)
    return level


def bell_draw(rng, extent, scale, bound, cuts=(), held_as=jnp.bfloat16):
    result = jax.random.normal(rng, extent, jnp.float32) * scale
    if len(cuts) > 0:
        result = block_levels(rng, extent, cuts, -0.22, 0.18) * result
    return jnp.clip(result, min=-bound, max=bound).astype(held_as)


def setup_inputs(seed: int = 0, part: int = 0) -> dict:
    key_list = jax.random.split(jax.random.key(seed), 11)
    part_keys = jax.random.split(jax.random.fold_in(key_list[10], part), 11)
    pair = bell_draw(part_keys[0], (N_TOK, N_TOK, C), 1.0, 6.0, ((0, 4), (1, 4)))
    mask = plant((jax.random.randint(part_keys[1], (N_TOK,), 0, 8) < 7).astype(jnp.int32), jax.random.fold_in(part_keys[1], 1), 0, 1)
    ln_gain = jnp.clip(jnp.exp(jax.random.uniform(key_list[2], (C,), jnp.float32, math.log(0.5), math.log(2.0))), 0.5, 2.0)
    ln_bias = bell_draw(key_list[3], (C,), 0.5, 3.0, (), jnp.float32)
    w_left = bell_draw(key_list[4], (C, 2 * CH), C ** -0.5, 0.5)
    w_right = bell_draw(key_list[5], (C, 2 * CH), C ** -0.5, 0.5)
    w_gate = bell_draw(key_list[6], (C, C), C ** -0.5, 0.5)
    w_out = bell_draw(key_list[7], (CH, C), CH ** -0.5, 0.5)
    out_gain = jnp.clip(jnp.exp(jax.random.uniform(key_list[8], (CH,), jnp.float32, math.log(0.5), math.log(2.0))), 0.5, 2.0)
    out_bias = bell_draw(key_list[9], (CH,), 0.5, 3.0, (), jnp.float32)
    return {"pair": pair, "mask": mask, "ln_gain": ln_gain, "ln_bias": ln_bias, "w_left": w_left, "w_right": w_right, "w_gate": w_gate, "w_out": w_out, "out_gain": out_gain, "out_bias": out_bias}


def layer_norm(values, scaling, shifting):
    average = lax.optimization_barrier(jnp.mean(values, axis=-1, keepdims=True))
    centered = values - average
    variance = lax.optimization_barrier(jnp.mean(centered * centered, axis=-1, keepdims=True))
    return centered * lax.rsqrt(variance + 1e-05) * scaling + shifting

def reference(pair, mask, ln_gain, ln_bias, w_left, w_right, w_gate, w_out, out_gain, out_bias):
    tokens = pair.shape[0]
    width = pair.shape[2]
    hidden_width = w_out.shape[0]
    validity = mask.astype(jnp.float32)
    cell_mask = (validity[:, None] * validity[None, :]).reshape(tokens * tokens, 1)
    normed = layer_norm(pair.astype(jnp.float32), ln_gain, ln_bias).astype(jnp.bfloat16)
    flattened = normed.reshape(tokens * tokens, width)

    def gated(weights):
        joined = jnp.dot(flattened, weights, preferred_element_type=jnp.float32)
        values = jax.nn.sigmoid(joined[:, hidden_width:]) * joined[:, :hidden_width] * cell_mask
        return values.astype(jnp.bfloat16).reshape(tokens, tokens, hidden_width)
    left = jnp.transpose(gated(w_left), (2, 0, 1)).astype(jnp.float32)
    right = jnp.transpose(gated(w_right), (2, 0, 1)).astype(jnp.float32)
    combined = jnp.einsum('cik,cjk->cij', left, right).astype(jnp.bfloat16)
    combined = jnp.transpose(combined, (1, 2, 0)).astype(jnp.float32)
    normed_out = layer_norm(combined, out_gain, out_bias).astype(jnp.bfloat16)
    gate_values = jax.nn.sigmoid(jnp.dot(flattened, w_gate, preferred_element_type=jnp.float32))
    projected = jnp.dot(normed_out.reshape(tokens * tokens, hidden_width), w_out, preferred_element_type=jnp.float32)
    return (gate_values * projected).reshape(tokens, tokens, width).astype(jnp.bfloat16)
```

```python
import functools

import jax
import jax.numpy as jnp
from jax import lax
from jax.experimental import pallas as pl
from jax.experimental.pallas import tpu as pltpu
from jax.sharding import PartitionSpec as P

MESH = pl.DeviceIdType.MESH
NT = (((1,), (1,)), ((), ()))
TN = (((0,), (0,)), ((), ()))
LIMIT = 56 * 1024 * 1024


def halves(a, b, half):
    low = jnp.concatenate([a[:, :half], b[:, :half]], axis=1)
    high = jnp.concatenate([a[:, half:], b[:, half:]], axis=1)
    return low, high


def project(steps, pair_ref, mask_ref, gain_ref, bias_ref, side_ref, wg_ref, left_ref, right_ref, gate_ref, scratch):
    folds, depth, cols, width = pair_ref.shape
    lanes = folds * cols
    hidden = side_ref.shape[0] // 4
    gain, bias = gain_ref[...], bias_ref[...]

    def step(n, carry):
        t0 = n * steps
        rows = [pair_ref[p, t0 + s] for s in range(steps) for p in range(folds)]
        x = jnp.concatenate(rows, axis=0).astype(jnp.float32)
        x = x - jnp.mean(x, axis=1, keepdims=True)
        x = x * lax.rsqrt(jnp.mean(x * x, axis=1, keepdims=True) + 1e-05) * gain + bias
        x = x.astype(jnp.bfloat16)
        gate = jax.nn.sigmoid(jnp.dot(x, wg_ref[...], preferred_element_type=jnp.float32))
        for s in range(steps):
            gate_ref[t0 + s] = gate[s * lanes : (s + 1) * lanes]
        for side in range(2):
            weights = side_ref[side * 2 * hidden : (side + 1) * 2 * hidden]
            joined = lax.dot_general(weights, x, NT, preferred_element_type=jnp.float32)
            for s in range(steps):
                part = joined[:, s * lanes : (s + 1) * lanes]
                value = jax.nn.sigmoid(part[hidden:]) * part[:hidden] * mask_ref[pl.ds(t0 + s, 1), :]
                scratch[side, pl.ds(t0 + s, hidden, stride=depth), :] = value
        return carry

    lax.fori_loop(0, depth // steps, step, 0)
    for side, ref in enumerate((left_ref, right_ref)):
        block = ref.shape[2]

        def cast(n, carry, side=side, ref=ref, block=block):
            at = pl.multiple_of(n * block, block)
            ref[n // ref.shape[1], n % ref.shape[1]] = scratch[side, pl.ds(at, block), :].astype(jnp.bfloat16)
            return carry

        lax.fori_loop(0, ref.shape[0] * ref.shape[1], cast, 0)


def exchange(plan, left_ref, right_ref, out_ref, lbuf, rbuf, sbuf, lsend, rsend, ssend, lrecv, rrecv, crecv):
    nrow, ncol, nh, nu, depth = plan
    per_half = nrow // nh
    me_row, me_col = lax.axis_index("row"), lax.axis_index("col")
    my_half = me_row // per_half
    rows = left_ref.shape[2]
    units = rows // depth

    def owner(h, u):
        if nh == 1:
            return u
        return jnp.where(u == 0, h * (nrow - 1), h + per_half - 1)

    def slot(u):
        return u * 0 if nh == 1 else jnp.maximum(u - 1, 0)

    if nh == 1:
        first, count = me_row, 1
    else:
        inner = jnp.logical_and(me_row > 0, me_row < nrow - 1)
        first, count = jnp.where(inner, 1, 0), jnp.where(inner, nu - 1, 1)

    barrier = pltpu.get_barrier_semaphore()
    others = nrow * ncol - 1

    def greet(n, carry):
        at = lax.rem(me_row * ncol + me_col + 1 + n, nrow * ncol)
        pl.semaphore_signal(barrier, 1, device_id={"row": at // ncol, "col": at % ncol}, device_id_type=MESH)
        return carry

    lax.fori_loop(0, others, greet, 0)
    pl.semaphore_wait(barrier, others)

    def move(row, col, src, dst, send, recv, begin):
        same = jnp.logical_and(row == me_row, col == me_col)
        remote = pltpu.make_async_remote_copy(
            src_ref=src, dst_ref=dst, send_sem=send, recv_sem=recv,
            device_id={"row": row, "col": col}, device_id_type=MESH,
        )

        @pl.when(jnp.logical_not(same))
        def _():
            if begin:
                remote.start()
            else:
                remote.wait_send()

        if begin:
            @pl.when(same)
            def _():
                pltpu.make_async_copy(src, dst, recv).start()

    def spread(begin):
        def body(n, carry):
            u = n // ncol
            col = lax.rem(me_col + n, ncol)
            m = slot(u)
            move(owner(my_half, u), col, left_ref.at[col, u], lbuf.at[m, me_row % per_half, me_col],
                 lsend.at[n], lrecv.at[m], begin)
            for d in range(nh):
                h = lax.rem(my_half + 1 + d, nh)
                move(owner(h, u), col, right_ref.at[col, u], rbuf.at[m, me_row, me_col],
                     rsend.at[n * nh + d], rrecv.at[m], begin)
            return carry

        lax.fori_loop(0, nu * ncol, body, 0)

    spread(True)

    def give(m, begin):
        def body(n, carry):
            b, col = n // ncol, lax.rem(me_col + n, ncol)
            move(my_half * per_half + b, col, sbuf.at[m, b, col], out_ref.at[me_col, first + m],
                 ssend.at[m * per_half * ncol + n], crecv, begin)
            return carry

        lax.fori_loop(0, per_half * ncol, body, 0)

    half = 64

    def gather(buf, m, blocks, at):
        strips = []
        for b in range(blocks):
            low, high = [], []
            for q in range(0, ncol, 2):
                lo, hi = halves(buf[m, b, q, pl.ds(at, depth), :], buf[m, b, q + 1, pl.ds(at, depth), :], half)
                low.append(lo)
                high.append(hi)
            strips += [jnp.concatenate(low, axis=1), jnp.concatenate(high, axis=1)]
        return jnp.concatenate(strips, axis=0)

    def work(m, carry):
        pltpu.make_async_copy(lbuf.at[m], lbuf.at[m], lrecv.at[m]).wait()
        pltpu.make_async_copy(rbuf.at[m], rbuf.at[m], rrecv.at[m]).wait()

        def channel(c, carry):
            at = pl.multiple_of(c * depth, depth)
            a = gather(lbuf, m, per_half, at)
            b = gather(rbuf, m, nrow, at)
            d = lax.dot_general(a, b, NT, preferred_element_type=jnp.float32).astype(jnp.bfloat16)
            for blk in range(per_half):
                top = d[blk * 2 * depth : blk * 2 * depth + depth]
                low = d[blk * 2 * depth + depth : (blk + 1) * 2 * depth]
                for q in range(0, ncol, 2):
                    span = slice(q * half, (q + 2) * half)
                    lo, hi = halves(top[:, span], low[:, span], half)
                    sbuf[m, blk, q, pl.ds(at, depth), :] = lo
                    sbuf[m, blk, q + 1, pl.ds(at, depth), :] = hi
            return carry

        lax.fori_loop(0, units, channel, 0)
        give(m, True)
        return carry

    lax.fori_loop(0, count, work, 0)
    pltpu.make_async_copy(out_ref, out_ref, crecv).wait()
    spread(False)

    def finish(m, carry):
        give(m, False)
        return carry

    lax.fori_loop(0, count, finish, 0)


def output(plane_ref, gate_ref, gain_ref, bias_ref, wo_ref, out_ref, scratch):
    folds, depth, cols, width = out_ref.shape
    hidden = wo_ref.shape[0]
    block = 512

    def cast(n, carry):
        at = pl.multiple_of(n * block, block)
        scratch[pl.ds(at, block), :] = plane_ref[pl.ds(at, block), :].astype(jnp.float32)
        return carry

    lax.fori_loop(0, hidden * depth // block, cast, 0)

    def step(t, carry):
        x = scratch[pl.ds(t, hidden, stride=depth), :]
        x = x - jnp.mean(x, axis=0, keepdims=True)
        x = x * lax.rsqrt(jnp.mean(x * x, axis=0, keepdims=True) + 1e-05) * gain_ref[...] + bias_ref[...]
        y = lax.dot_general(x.astype(jnp.bfloat16), wo_ref[...], TN, preferred_element_type=jnp.float32)
        y = (y * gate_ref[t]).astype(jnp.bfloat16)
        for p in range(folds):
            out_ref[p, t] = y[p * cols : (p + 1) * cols]
        return carry

    lax.fori_loop(0, depth, step, 0, unroll=2)


def body(nrow, ncol, pair, mask, ln_gain, ln_bias, w_left, w_right, w_gate, w_out, out_gain, out_bias):
    tile_rows, tile_cols, width = pair.shape
    hidden = w_out.shape[0]
    lanes = 128
    folds = lanes // tile_cols
    depth = tile_rows // folds
    nh, nu = (2, 4) if nrow == 4 else (1, nrow)
    slots = nu - 1 if nh == 2 else 1
    per_half = nrow // nh
    rows = hidden // (ncol * nu) * depth
    validity = mask.astype(jnp.float32)
    row_valid = lax.dynamic_slice_in_dim(validity, lax.axis_index("row") * tile_rows, tile_rows)
    col_valid = lax.dynamic_slice_in_dim(validity, lax.axis_index("col") * tile_cols, tile_cols)
    cells = row_valid.reshape(folds, depth).T[:, :, None] * col_valid[None, None, :]
    cells = cells.reshape(depth, lanes)
    side_weights = jnp.concatenate([w_left, w_right], axis=1).T
    vmem = pl.BlockSpec(memory_space=pltpu.VMEM)
    anywhere = pl.BlockSpec(memory_space=pl.ANY)
    packed = jax.ShapeDtypeStruct((ncol, nu, rows, lanes), jnp.bfloat16)
    left, right, gate = pl.pallas_call(
        functools.partial(project, 4),
        out_shape=(packed, packed, jax.ShapeDtypeStruct((depth, lanes, width), jnp.float32)),
        in_specs=[vmem] * 6,
        out_specs=(vmem,) * 3,
        scratch_shapes=[pltpu.VMEM((2, hidden * depth, lanes), jnp.float32)],
        compiler_params=pltpu.CompilerParams(vmem_limit_bytes=LIMIT),
    )(
        pair.reshape(folds, depth, tile_cols, width), cells,
        ln_gain.reshape(1, width), ln_bias.reshape(1, width), side_weights, w_gate,
    )
    plane = pl.pallas_call(
        functools.partial(exchange, (nrow, ncol, nh, nu, depth)),
        out_shape=packed,
        in_specs=[anywhere] * 2,
        out_specs=anywhere,
        scratch_shapes=[
            pltpu.VMEM((slots, per_half, ncol, rows, lanes), jnp.bfloat16),
            pltpu.VMEM((slots, nrow, ncol, rows, lanes), jnp.bfloat16),
            pltpu.VMEM((slots, per_half, ncol, rows, lanes), jnp.bfloat16),
            pltpu.SemaphoreType.DMA((nu * ncol,)),
            pltpu.SemaphoreType.DMA((nu * ncol * nh,)),
            pltpu.SemaphoreType.DMA((slots * per_half * ncol,)),
            pltpu.SemaphoreType.DMA((slots,)),
            pltpu.SemaphoreType.DMA((slots,)),
            pltpu.SemaphoreType.DMA,
        ],
        compiler_params=pltpu.CompilerParams(
            collective_id=0, has_side_effects=True, vmem_limit_bytes=LIMIT
        ),
    )(left, right)
    out = pl.pallas_call(
        output,
        out_shape=jax.ShapeDtypeStruct((folds, depth, tile_cols, width), jnp.bfloat16),
        in_specs=[vmem] * 5,
        out_specs=vmem,
        scratch_shapes=[pltpu.VMEM((hidden * depth, lanes), jnp.float32)],
        compiler_params=pltpu.CompilerParams(vmem_limit_bytes=LIMIT),
    )(
        plane.reshape(hidden * depth, lanes), gate,
        jnp.broadcast_to(out_gain[:, None], (hidden, lanes)),
        jnp.broadcast_to(out_bias[:, None], (hidden, lanes)), w_out,
    )
    return out.reshape(tile_rows, tile_cols, width)


def solution(mesh):
    return jax.shard_map(
        functools.partial(body, mesh.shape["row"], mesh.shape["col"]),
        mesh=mesh,
        in_specs=(P(("groups", "row"), "col", None), P("groups"), P(), P(), P(), P(), P(), P(), P(), P()),
        out_specs=P(("groups", "row"), "col", None),
        check_vma=False,
    )
```

```python
import functools

import jax
import jax.numpy as jnp
from jax import lax
from jax.experimental import pallas as pl
from jax.experimental.pallas import tpu as pltpu
from jax.sharding import PartitionSpec as P

MESH = pl.DeviceIdType.MESH
NT = (((1,), (1,)), ((), ()))
TN = (((0,), (0,)), ((), ()))
LIMIT = 56 * 1024 * 1024


def halves(a, b, half):
    low = jnp.concatenate([a[:, :half], b[:, :half]], axis=1)
    high = jnp.concatenate([a[:, half:], b[:, half:]], axis=1)
    return low, high


def project(steps, pair_ref, flag_ref, cols_ref, gain_ref, bias_ref, wl_ref, wr_ref, wg_ref, left_ref, right_ref, gate_ref, scratch):
    folds, depth, cols, width = pair_ref.shape
    lanes = folds * cols
    hidden = wl_ref.shape[1] // 2
    gain, bias = gain_ref[...], bias_ref[...]
    sides = [ref[...].astype(jnp.float32).T.astype(jnp.bfloat16) for ref in (wl_ref, wr_ref)]
    first_row = lax.axis_index("row") * (folds * depth)
    col_valid = cols_ref[pl.ds(lax.axis_index("col"), 1), :].astype(jnp.float32)
    col_valid = jnp.concatenate([col_valid] * folds, axis=1)
    fold = lax.broadcasted_iota(jnp.int32, (1, lanes), 1) // cols

    def valid(t):
        flags = flag_ref[first_row + t]
        for p in range(1, folds):
            flags = jnp.where(fold == p, flag_ref[first_row + p * depth + t], flags)
        return col_valid * flags.astype(jnp.float32)

    def step(n, carry):
        t0 = n * steps
        rows = [pair_ref[p, t0 + s] for s in range(steps) for p in range(folds)]
        x = jnp.concatenate(rows, axis=0).astype(jnp.float32)
        x = x - jnp.mean(x, axis=1, keepdims=True)
        x = x * lax.rsqrt(jnp.mean(x * x, axis=1, keepdims=True) + 1e-05) * gain + bias
        x = x.astype(jnp.bfloat16)
        gate = jax.nn.sigmoid(jnp.dot(x, wg_ref[...], preferred_element_type=jnp.float32))
        for s in range(steps):
            gate_ref[t0 + s] = gate[s * lanes : (s + 1) * lanes]
        valids = [valid(t0 + s) for s in range(steps)]
        for side in range(2):
            joined = lax.dot_general(sides[side], x, NT, preferred_element_type=jnp.float32)
            for s in range(steps):
                part = joined[:, s * lanes : (s + 1) * lanes]
                value = jax.nn.sigmoid(part[hidden:]) * part[:hidden] * valids[s]
                scratch[side, pl.ds(t0 + s, hidden, stride=depth), :] = value
        return carry

    lax.fori_loop(0, depth // steps, step, 0)
    for side, ref in enumerate((left_ref, right_ref)):
        block = ref.shape[2]

        def cast(n, carry, side=side, ref=ref, block=block):
            at = pl.multiple_of(n * block, block)
            ref[n // ref.shape[1], n % ref.shape[1]] = scratch[side, pl.ds(at, block), :].astype(jnp.bfloat16)
            return carry

        lax.fori_loop(0, ref.shape[0] * ref.shape[1], cast, 0)


def exchange(plan, left_ref, right_ref, out_ref, lbuf, rbuf, sbuf, lsend, rsend, ssend, lrecv, rrecv, crecv, relays):
    nrow, ncol, nh, nu, depth = plan
    per_half = nrow // nh
    me_row, me_col = lax.axis_index("row"), lax.axis_index("col")
    my_half = me_row // per_half
    rows = left_ref.shape[2]
    units = rows // depth
    slots = lbuf.shape[0]

    def owner(h, u):
        if nh == 1:
            return u
        return jnp.where(u == 0, h * (nrow - 1), h + per_half - 1)

    def slot(u):
        return u * 0 if nh == 1 else jnp.maximum(u - 1, 0)

    if nh == 1:
        first, count = me_row, 1
    else:
        inner = jnp.logical_and(me_row > 0, me_row < nrow - 1)
        first, count = jnp.where(inner, 1, 0), jnp.where(inner, nu - 1, 1)

    barrier = pltpu.get_barrier_semaphore()
    others = nrow * ncol - 1

    def greet(n, carry):
        at = lax.rem(me_row * ncol + me_col + 1 + n, nrow * ncol)
        pl.semaphore_signal(barrier, 1, device_id={"row": at // ncol, "col": at % ncol}, device_id_type=MESH)
        return carry

    lax.fori_loop(0, others, greet, 0)
    pl.semaphore_wait(barrier, others)

    def move(row, col, src, dst, send, recv, begin, wanted=True):
        same = jnp.logical_and(row == me_row, col == me_col)
        remote = pltpu.make_async_remote_copy(
            src_ref=src, dst_ref=dst, send_sem=send, recv_sem=recv,
            device_id={"row": row, "col": col}, device_id_type=MESH,
        )

        @pl.when(jnp.logical_and(jnp.logical_not(same), wanted))
        def _():
            if begin:
                remote.start()
            else:
                remote.wait_send()

        if begin:
            @pl.when(same)
            def _():
                pltpu.make_async_copy(src, dst, recv).start()

    def spread(begin):
        def rights(n, carry):
            u = n // ncol
            col = lax.rem(me_col + n, ncol)
            m = slot(u)
            for d in range(nh):
                h = lax.rem(my_half + 1 + d, nh)
                wanted = True
                if nh == 2 and d == 0:
                    wanted = jnp.logical_or(inner, u == 0)
                move(owner(h, u), col, right_ref.at[col, u], rbuf.at[m, me_row, me_col],
                     rsend.at[n * nh + d], rrecv.at[m, me_row], begin, wanted)
            return carry

        def lefts(n, carry):
            u = n // ncol
            col = lax.rem(me_col + n, ncol)
            m = slot(u)
            move(owner(my_half, u), col, left_ref.at[col, u], lbuf.at[m, me_row % per_half, me_col],
                 lsend.at[n], lrecv.at[m], begin)
            return carry

        lax.fori_loop(0, nu * ncol, rights, 0)
        lax.fori_loop(0, nu * ncol, lefts, 0)

    def take(m, row):
        pltpu.make_async_copy(rbuf.at[m, row], rbuf.at[m, row], rrecv.at[m, row]).wait()

    outer = my_half * (nrow - 1)
    across = nrow - 1 - me_row

    def relay(begin):
        def body(m, carry):
            copy = pltpu.make_async_remote_copy(
                src_ref=rbuf.at[m, outer], dst_ref=rbuf.at[m, outer], send_sem=relays.at[m],
                recv_sem=rrecv.at[m, outer], device_id={"row": across}, device_id_type=MESH,
            )
            if begin:
                take(m, outer)
                copy.start()
            else:
                copy.wait_send()
            return carry

        @pl.when(inner)
        def _():
            lax.fori_loop(0, slots, body, 0)

    spread(True)
    if nh == 2:
        relay(True)

    def give(m, begin):
        def body(n, carry):
            b, col = n // ncol, lax.rem(me_col + n, ncol)
            move(my_half * per_half + b, col, sbuf.at[m, b, col], out_ref.at[me_col, first + m],
                 ssend.at[m * per_half * ncol + n], crecv, begin)
            return carry

        lax.fori_loop(0, per_half * ncol, body, 0)

    half = 64

    def gather(buf, m, blocks, at):
        strips = []
        for b in range(blocks):
            low, high = [], []
            for q in range(0, ncol, 2):
                lo, hi = halves(buf[m, b, q, pl.ds(at, depth), :], buf[m, b, q + 1, pl.ds(at, depth), :], half)
                low.append(lo)
                high.append(hi)
            strips += [jnp.concatenate(low, axis=1), jnp.concatenate(high, axis=1)]
        return jnp.concatenate(strips, axis=0)

    def work(m, carry):
        pltpu.make_async_copy(lbuf.at[m], lbuf.at[m], lrecv.at[m]).wait()
        for row in range(nrow):
            if nh == 2:
                pl.when(jnp.logical_not(jnp.logical_and(inner, row == outer)))(functools.partial(take, m, row))
            else:
                take(m, row)

        def channel(c, carry):
            at = pl.multiple_of(c * depth, depth)
            a = gather(lbuf, m, per_half, at)
            b = gather(rbuf, m, nrow, at)
            d = lax.dot_general(a, b, NT, preferred_element_type=jnp.float32).astype(jnp.bfloat16)
            for blk in range(per_half):
                top = d[blk * 2 * depth : blk * 2 * depth + depth]
                low = d[blk * 2 * depth + depth : (blk + 1) * 2 * depth]
                for q in range(0, ncol, 2):
                    span = slice(q * half, (q + 2) * half)
                    lo, hi = halves(top[:, span], low[:, span], half)
                    sbuf[m, blk, q, pl.ds(at, depth), :] = lo
                    sbuf[m, blk, q + 1, pl.ds(at, depth), :] = hi
            return carry

        lax.fori_loop(0, units, channel, 0)
        give(m, True)
        return carry

    lax.fori_loop(0, count, work, 0)
    pltpu.make_async_copy(out_ref, out_ref, crecv).wait()
    spread(False)
    if nh == 2:
        relay(False)

    def finish(m, carry):
        give(m, False)
        return carry

    lax.fori_loop(0, count, finish, 0)


def output(plane_ref, gate_ref, gain_ref, bias_ref, wo_ref, out_ref, scratch):
    folds, depth, cols, width = out_ref.shape
    hidden = wo_ref.shape[0]
    block = 512
    gain, bias = (jnp.broadcast_to(ref[...], (folds * cols, hidden)).T for ref in (gain_ref, bias_ref))

    def cast(n, carry):
        at = pl.multiple_of(n * block, block)
        scratch[pl.ds(at, block), :] = plane_ref[pl.ds(at, block), :].astype(jnp.float32)
        return carry

    lax.fori_loop(0, hidden * depth // block, cast, 0)

    def step(t, carry):
        x = scratch[pl.ds(t, hidden, stride=depth), :]
        x = x - jnp.mean(x, axis=0, keepdims=True)
        x = x * lax.rsqrt(jnp.mean(x * x, axis=0, keepdims=True) + 1e-05) * gain + bias
        y = lax.dot_general(x.astype(jnp.bfloat16), wo_ref[...], TN, preferred_element_type=jnp.float32)
        y = (y * gate_ref[t]).astype(jnp.bfloat16)
        for p in range(folds):
            out_ref[p, t] = y[p * cols : (p + 1) * cols]
        return carry

    lax.fori_loop(0, depth, step, 0, unroll=2)


def body(nrow, ncol, pair, mask, ln_gain, ln_bias, w_left, w_right, w_gate, w_out, out_gain, out_bias):
    tile_rows, tile_cols, width = pair.shape
    hidden = w_out.shape[0]
    lanes = 128
    folds = lanes // tile_cols
    depth = tile_rows // folds
    nh, nu = (2, 4) if nrow == 4 else (1, nrow)
    slots = nu - 1 if nh == 2 else 1
    per_half = nrow // nh
    rows = hidden // (ncol * nu) * depth
    vmem = pl.BlockSpec(memory_space=pltpu.VMEM)
    anywhere = pl.BlockSpec(memory_space=pl.ANY)
    packed = jax.ShapeDtypeStruct((ncol, nu, rows, lanes), jnp.bfloat16)
    left, right, gate = pl.pallas_call(
        functools.partial(project, 4),
        out_shape=(packed, packed, jax.ShapeDtypeStruct((depth, lanes, width), jnp.float32)),
        in_specs=[vmem, pl.BlockSpec(memory_space=pltpu.SMEM)] + [vmem] * 6,
        out_specs=(vmem,) * 3,
        scratch_shapes=[pltpu.VMEM((2, hidden * depth, lanes), jnp.float32)],
        compiler_params=pltpu.CompilerParams(vmem_limit_bytes=LIMIT),
    )(
        pair.reshape(folds, depth, tile_cols, width), mask, mask.reshape(ncol, tile_cols),
        ln_gain.reshape(1, width), ln_bias.reshape(1, width), w_left, w_right, w_gate,
    )
    plane = pl.pallas_call(
        functools.partial(exchange, (nrow, ncol, nh, nu, depth)),
        out_shape=packed,
        in_specs=[anywhere] * 2,
        out_specs=anywhere,
        scratch_shapes=[
            pltpu.VMEM((slots, per_half, ncol, rows, lanes), jnp.bfloat16),
            pltpu.VMEM((slots, nrow, ncol, rows, lanes), jnp.bfloat16),
            pltpu.VMEM((slots, per_half, ncol, rows, lanes), jnp.bfloat16),
            pltpu.SemaphoreType.DMA((nu * ncol,)),
            pltpu.SemaphoreType.DMA((nu * ncol * nh,)),
            pltpu.SemaphoreType.DMA((slots * per_half * ncol,)),
            pltpu.SemaphoreType.DMA((slots,)),
            pltpu.SemaphoreType.DMA((slots, nrow)),
            pltpu.SemaphoreType.DMA,
            pltpu.SemaphoreType.DMA((slots,)),
        ],
        compiler_params=pltpu.CompilerParams(
            collective_id=0, has_side_effects=True, vmem_limit_bytes=LIMIT
        ),
    )(left, right)
    out = pl.pallas_call(
        output,
        out_shape=jax.ShapeDtypeStruct((folds, depth, tile_cols, width), jnp.bfloat16),
        in_specs=[vmem] * 5,
        out_specs=vmem,
        scratch_shapes=[pltpu.VMEM((hidden * depth, lanes), jnp.float32)],
        compiler_params=pltpu.CompilerParams(vmem_limit_bytes=LIMIT),
    )(
        plane.reshape(hidden * depth, lanes), gate,
        out_gain.reshape(1, hidden), out_bias.reshape(1, hidden), w_out,
    )
    return out.reshape(tile_rows, tile_cols, width)


def solution(mesh):
    return jax.shard_map(
        functools.partial(body, mesh.shape["row"], mesh.shape["col"]),
        mesh=mesh,
        in_specs=(P(("groups", "row"), "col", None), P("groups"), P(), P(), P(), P(), P(), P(), P(), P()),
        out_specs=P(("groups", "row"), "col", None),
        check_vma=False,
    )
```

```python
import functools

import jax
import jax.numpy as jnp
from jax import lax
from jax.experimental import pallas as pl
from jax.experimental.pallas import tpu as pltpu
from jax.sharding import PartitionSpec as P

MESH = pl.DeviceIdType.MESH
NT = (((1,), (1,)), ((), ()))
TN = (((0,), (0,)), ((), ()))
LIMIT = 56 * 1024 * 1024


def halves(a, b, half):
    low = jnp.concatenate([a[:, :half], b[:, :half]], axis=1)
    high = jnp.concatenate([a[:, half:], b[:, half:]], axis=1)
    return low, high


def project(steps, pair_ref, flag_ref, cols_ref, gain_ref, bias_ref, wl_ref, wr_ref, wg_ref, left_ref, right_ref, gate_ref, scratch):
    folds, depth, cols, width = pair_ref.shape
    lanes = folds * cols
    hidden = wl_ref.shape[1] // 2
    gain, bias = gain_ref[...], bias_ref[...]
    sides = [ref[...].astype(jnp.float32).T.astype(jnp.bfloat16) for ref in (wl_ref, wr_ref)]
    first_row = lax.axis_index("row") * (folds * depth)
    col_valid = cols_ref[pl.ds(lax.axis_index("col"), 1), :].astype(jnp.float32)
    col_valid = jnp.concatenate([col_valid] * folds, axis=1)
    fold = lax.broadcasted_iota(jnp.int32, (1, lanes), 1) // cols

    def valid(t):
        flags = flag_ref[first_row + t]
        for p in range(1, folds):
            flags = jnp.where(fold == p, flag_ref[first_row + p * depth + t], flags)
        return col_valid * flags.astype(jnp.float32)

    def step(n, carry):
        t0 = n * steps
        rows = [pair_ref[p, t0 + s] for s in range(steps) for p in range(folds)]
        x = jnp.concatenate(rows, axis=0).astype(jnp.float32)
        x = x - jnp.mean(x, axis=1, keepdims=True)
        x = x * lax.rsqrt(jnp.mean(x * x, axis=1, keepdims=True) + 1e-05) * gain + bias
        x = x.astype(jnp.bfloat16)
        gate = jax.nn.sigmoid(jnp.dot(x, wg_ref[...], preferred_element_type=jnp.float32))
        for s in range(steps):
            gate_ref[t0 + s] = gate[s * lanes : (s + 1) * lanes]
        valids = [valid(t0 + s) for s in range(steps)]
        for side in range(2):
            joined = lax.dot_general(sides[side], x, NT, preferred_element_type=jnp.float32)
            for s in range(steps):
                part = joined[:, s * lanes : (s + 1) * lanes]
                value = jax.nn.sigmoid(part[hidden:]) * part[:hidden] * valids[s]
                scratch[side, pl.ds(t0 + s, hidden, stride=depth), :] = value
        return carry

    lax.fori_loop(0, depth // steps, step, 0)
    for side, ref in enumerate((left_ref, right_ref)):
        block = ref.shape[2]

        def cast(n, carry, side=side, ref=ref, block=block):
            at = pl.multiple_of(n * block, block)
            ref[n // ref.shape[1], n % ref.shape[1]] = scratch[side, pl.ds(at, block), :].astype(jnp.bfloat16)
            return carry

        lax.fori_loop(0, ref.shape[0] * ref.shape[1], cast, 0)


def exchange(plan, left_ref, right_ref, out_ref, lbuf, rbuf, sbuf, lsend, rsend, ssend, lrecv, rrecv, crecv, relays):
    nrow, ncol, nh, nu, depth = plan
    per_half = nrow // nh
    me_row, me_col = lax.axis_index("row"), lax.axis_index("col")
    my_half = me_row // per_half
    rows = left_ref.shape[2]
    units = rows // depth
    slots = lbuf.shape[0]

    def owner(h, u):
        if nh == 1:
            return u
        return jnp.where(u == 0, h * (nrow - 1), h + per_half - 1)

    def slot(u):
        return u * 0 if nh == 1 else jnp.maximum(u - 1, 0)

    if nh == 1:
        first, count = me_row, 1
    else:
        inner = jnp.logical_and(me_row > 0, me_row < nrow - 1)
        first, count = jnp.where(inner, 1, 0), jnp.where(inner, nu - 1, 1)

    barrier = pltpu.get_barrier_semaphore()
    others = nrow * ncol - 1

    def greet(n, carry):
        at = lax.rem(me_row * ncol + me_col + 1 + n, nrow * ncol)
        pl.semaphore_signal(barrier, 1, device_id={"row": at // ncol, "col": at % ncol}, device_id_type=MESH)
        return carry

    lax.fori_loop(0, others, greet, 0)
    pl.semaphore_wait(barrier, others)

    def move(row, col, src, dst, send, recv, begin, wanted=True):
        same = jnp.logical_and(row == me_row, col == me_col)
        remote = pltpu.make_async_remote_copy(
            src_ref=src, dst_ref=dst, send_sem=send, recv_sem=recv,
            device_id={"row": row, "col": col}, device_id_type=MESH,
        )

        @pl.when(jnp.logical_and(jnp.logical_not(same), wanted))
        def _():
            if begin:
                remote.start()
            else:
                remote.wait_send()

        if begin:
            @pl.when(same)
            def _():
                pltpu.make_async_copy(src, dst, recv).start()

    def spread(begin):
        def rights(n, carry):
            u = n // ncol
            col = lax.rem(me_col + n, ncol)
            m = slot(u)
            for d in range(nh):
                h = lax.rem(my_half + 1 + d, nh)
                wanted = True
                if nh == 2 and d == 0:
                    wanted = jnp.logical_or(inner, u == 0)
                move(owner(h, u), col, right_ref.at[col, u], rbuf.at[m, me_row, me_col],
                     rsend.at[n * nh + d], rrecv.at[m, me_row], begin, wanted)
            return carry

        def lefts(n, carry):
            u = n // ncol
            col = lax.rem(me_col + n, ncol)
            m = slot(u)
            move(owner(my_half, u), col, left_ref.at[col, u], lbuf.at[m, me_row % per_half, me_col],
                 lsend.at[n], lrecv.at[m], begin)
            return carry

        lax.fori_loop(0, nu * ncol, rights, 0)
        lax.fori_loop(0, nu * ncol, lefts, 0)

    def take(m, row):
        pltpu.make_async_copy(rbuf.at[m, row], rbuf.at[m, row], rrecv.at[m, row]).wait()

    outer = my_half * (nrow - 1)
    across = nrow - 1 - me_row

    def relay(begin):
        def body(m, carry):
            copy = pltpu.make_async_remote_copy(
                src_ref=rbuf.at[m, outer], dst_ref=rbuf.at[m, outer], send_sem=relays.at[m],
                recv_sem=rrecv.at[m, outer], device_id={"row": across}, device_id_type=MESH,
            )
            if begin:
                take(m, outer)
                copy.start()
            else:
                copy.wait_send()
            return carry

        @pl.when(inner)
        def _():
            lax.fori_loop(0, slots, body, 0)

    spread(True)
    if nh == 2:
        relay(True)

    def give(m, begin):
        def body(n, carry):
            b, col = n // ncol, lax.rem(me_col + n, ncol)
            move(my_half * per_half + b, col, sbuf.at[m, b, col], out_ref.at[me_col, first + m],
                 ssend.at[m * per_half * ncol + n], crecv, begin)
            return carry

        lax.fori_loop(0, per_half * ncol, body, 0)

    half = 64

    def gather(buf, m, blocks, at):
        strips = []
        for b in range(blocks):
            low, high = [], []
            for q in range(0, ncol, 2):
                lo, hi = halves(buf[m, b, q, pl.ds(at, depth), :], buf[m, b, q + 1, pl.ds(at, depth), :], half)
                low.append(lo)
                high.append(hi)
            strips += [jnp.concatenate(low, axis=1), jnp.concatenate(high, axis=1)]
        return jnp.concatenate(strips, axis=0)

    def work(m, carry):
        pltpu.make_async_copy(lbuf.at[m], lbuf.at[m], lrecv.at[m]).wait()
        for row in range(nrow):
            if nh == 2:
                pl.when(jnp.logical_not(jnp.logical_and(inner, row == outer)))(functools.partial(take, m, row))
            else:
                take(m, row)

        def channel(c, carry):
            at = pl.multiple_of(c * depth, depth)
            a = gather(lbuf, m, per_half, at)
            b = gather(rbuf, m, nrow, at)
            d = lax.dot_general(a, b, NT, preferred_element_type=jnp.float32).astype(jnp.bfloat16)
            for blk in range(per_half):
                top = d[blk * 2 * depth : blk * 2 * depth + depth]
                low = d[blk * 2 * depth + depth : (blk + 1) * 2 * depth]
                for q in range(0, ncol, 2):
                    span = slice(q * half, (q + 2) * half)
                    lo, hi = halves(top[:, span], low[:, span], half)
                    sbuf[m, blk, q, pl.ds(at, depth), :] = lo
                    sbuf[m, blk, q + 1, pl.ds(at, depth), :] = hi
            return carry

        lax.fori_loop(0, units, channel, 0)
        give(m, True)
        return carry

    lax.fori_loop(0, count, work, 0)
    pltpu.make_async_copy(out_ref, out_ref, crecv).wait()
    spread(False)
    if nh == 2:
        relay(False)

    def finish(m, carry):
        give(m, False)
        return carry

    lax.fori_loop(0, count, finish, 0)


def output(plane_ref, gate_ref, gain_ref, bias_ref, wo_ref, out_ref, scratch):
    folds, depth, cols, width = out_ref.shape
    hidden = wo_ref.shape[0]
    block = 512
    gain, bias = (jnp.broadcast_to(ref[...], (folds * cols, hidden)).T for ref in (gain_ref, bias_ref))

    def cast(n, carry):
        at = pl.multiple_of(n * block, block)
        scratch[pl.ds(at, block), :] = plane_ref[pl.ds(at, block), :].astype(jnp.float32)
        return carry

    lax.fori_loop(0, hidden * depth // block, cast, 0)

    def step(t, carry):
        x = scratch[pl.ds(t, hidden, stride=depth), :]
        x = x - jnp.mean(x, axis=0, keepdims=True)
        x = x * lax.rsqrt(jnp.mean(x * x, axis=0, keepdims=True) + 1e-05) * gain + bias
        y = lax.dot_general(x.astype(jnp.bfloat16), wo_ref[...], TN, preferred_element_type=jnp.float32)
        y = (y * gate_ref[t]).astype(jnp.bfloat16)
        for p in range(folds):
            out_ref[p, t] = y[p * cols : (p + 1) * cols]
        return carry

    lax.fori_loop(0, depth, step, 0, unroll=4)


def body(nrow, ncol, pair, mask, ln_gain, ln_bias, w_left, w_right, w_gate, w_out, out_gain, out_bias):
    tile_rows, tile_cols, width = pair.shape
    hidden = w_out.shape[0]
    lanes = 128
    folds = lanes // tile_cols
    depth = tile_rows // folds
    nh, nu = (2, 4) if nrow == 4 else (1, nrow)
    slots = nu - 1 if nh == 2 else 1
    per_half = nrow // nh
    rows = hidden // (ncol * nu) * depth
    vmem = pl.BlockSpec(memory_space=pltpu.VMEM)
    anywhere = pl.BlockSpec(memory_space=pl.ANY)
    packed = jax.ShapeDtypeStruct((ncol, nu, rows, lanes), jnp.bfloat16)
    left, right, gate = pl.pallas_call(
        functools.partial(project, 8),
        out_shape=(packed, packed, jax.ShapeDtypeStruct((depth, lanes, width), jnp.float32)),
        in_specs=[vmem, pl.BlockSpec(memory_space=pltpu.SMEM)] + [vmem] * 6,
        out_specs=(vmem,) * 3,
        scratch_shapes=[pltpu.VMEM((2, hidden * depth, lanes), jnp.float32)],
        compiler_params=pltpu.CompilerParams(vmem_limit_bytes=LIMIT),
    )(
        pair.reshape(folds, depth, tile_cols, width), mask, mask.reshape(ncol, tile_cols),
        ln_gain.reshape(1, width), ln_bias.reshape(1, width), w_left, w_right, w_gate,
    )
    plane = pl.pallas_call(
        functools.partial(exchange, (nrow, ncol, nh, nu, depth)),
        out_shape=packed,
        in_specs=[anywhere] * 2,
        out_specs=anywhere,
        scratch_shapes=[
            pltpu.VMEM((slots, per_half, ncol, rows, lanes), jnp.bfloat16),
            pltpu.VMEM((slots, nrow, ncol, rows, lanes), jnp.bfloat16),
            pltpu.VMEM((slots, per_half, ncol, rows, lanes), jnp.bfloat16),
            pltpu.SemaphoreType.DMA((nu * ncol,)),
            pltpu.SemaphoreType.DMA((nu * ncol * nh,)),
            pltpu.SemaphoreType.DMA((slots * per_half * ncol,)),
            pltpu.SemaphoreType.DMA((slots,)),
            pltpu.SemaphoreType.DMA((slots, nrow)),
            pltpu.SemaphoreType.DMA,
            pltpu.SemaphoreType.DMA((slots,)),
        ],
        compiler_params=pltpu.CompilerParams(
            collective_id=0, has_side_effects=True, vmem_limit_bytes=LIMIT
        ),
    )(left, right)
    out = pl.pallas_call(
        output,
        out_shape=jax.ShapeDtypeStruct((folds, depth, tile_cols, width), jnp.bfloat16),
        in_specs=[vmem] * 5,
        out_specs=vmem,
        scratch_shapes=[pltpu.VMEM((hidden * depth, lanes), jnp.float32)],
        compiler_params=pltpu.CompilerParams(vmem_limit_bytes=LIMIT),
    )(
        plane.reshape(hidden * depth, lanes), gate,
        out_gain.reshape(1, hidden), out_bias.reshape(1, hidden), w_out,
    )
    return out.reshape(tile_rows, tile_cols, width)


def solution(mesh):
    return jax.shard_map(
        functools.partial(body, mesh.shape["row"], mesh.shape["col"]),
        mesh=mesh,
        in_specs=(P(("groups", "row"), "col", None), P("groups"), P(), P(), P(), P(), P(), P(), P(), P()),
        out_specs=P(("groups", "row"), "col", None),
        check_vma=False,
    )
```
